32 devices in a mesh: shard: 2 (over y), tensor: 4 (over z), section: 4 (over x, core).
Axes of the slice: x: 2, y: 2, z: 4, core: 2. Of those that a mesh axis runs over, the one named last changes fastest.
Arguments:
- activations: bfloat16 [4, 4096, 2048], P('section', 'shard'), may hold values from -500 to 500, as said below
- out_grad: bfloat16 [4, 4096, 8192], P('section', 'shard', 'tensor'), may hold values from -30 to 30, as said below
- basis: float32 [4, 2048, 256], P('section', 'shard'), may hold values from -0.125 to 0.125
- first_moment: float32 [4, 256, 8192], P('section', 'shard', 'tensor'), may hold values from -6 to 6
- second_moment: float32 [4, 256, 8192], P('section', 'shard', 'tensor'), may hold values from 0.5 to 2
- gain_partial: float32 [4, 2, 2048], P('section', 'shard'), may hold values from -4096 to 4096
- gain_first: float32 [4, 2048], P('section', 'shard'), may hold values from -6 to 6
- gain_second: float32 [4, 2048], P('section', 'shard'), may hold values from 0.5 to 2
Outputs:
- update: float32 [4, 2048, 8192], P('section', 'shard', 'tensor')
- first_out: float32 [4, 256, 8192], P('section', 'shard', 'tensor')
- second_out: float32 [4, 256, 8192], P('section', 'shard', 'tensor')
- new_basis: float32 [4, 2048, 256], P('section', ('shard', 'tensor'))
- gain_step: float32 [4, 2048], P('section', 'shard')
- gain_first_out: float32 [4, 2048], P('section', 'shard')
- gain_second_out: float32 [4, 2048], P('section', 'shard')
The draws below stay inside these ranges and needn't reach their ends.
Inputs may be any that keep to these rules, and one draw needn't show every extreme that they name: Real-valued activations whose column scales differ from column to column. `out_grad`: Real-valued gradients whose column scales differ from column to column.
All inputs are finite; a program needn't handle non-finite values.
Results may differ from the reference program's by a relative error of at most 0.0003.
Values sent between devices are 32-bit elements; how exact they have to be, the bound alone decides.
A program may use at most 128 MiB of HBM per device.

```python
import math
import jax
import jax.numpy as jnp
from jax import lax

D = 2048
FF = 8192
RANK = 256
TOK_DEV = 2048
NS_STEPS = 5
STEP = 8
LAYERS = 4
TOKENS = 4096
N_SHARD = 2


def draw_activations(key, part):
    key_values, key_columns = jax.random.split(key, 2)
    column_pos = jnp.arange(D, dtype=jnp.float32) / float(D)
    layer_pos = jnp.arange(LAYERS, dtype=jnp.float32) / float(max(LAYERS - 1, 1))
    random_scale = jnp.exp(jax.random.uniform(key_columns, (LAYERS, 1, D), jnp.float32) * math.log(10.0))
    rising = jnp.exp(1.1 * column_pos)
    column_scale = random_scale * rising[None, None, :] * jnp.exp(0.3 * layer_pos)[:, None, None]
    values = jnp.clip(jax.random.normal(key_values, (LAYERS, TOKENS, D), jnp.float32), -4.0, 4.0)
    return (values * column_scale).astype(jnp.bfloat16)


def draw_out_grad(key, part):
    key_values = jax.random.fold_in(key, 17)
    column_pos = jnp.arange(FF, dtype=jnp.float32) / float(FF)
    rising = jnp.exp(1.1 * column_pos)
    values = jnp.clip(jax.random.normal(key_values, (LAYERS, TOKENS, FF), jnp.float32), -5.0, 5.0)
    return (values * rising[None, None, :]).astype(jnp.bfloat16)


def levels(rng, shape, pieces, smallest, largest):
    def one(axis_at, shards_of):
        heights = jax.random.uniform(jax.random.fold_in(jax.random.fold_in(rng, 6), axis_at), (shards_of,), jnp.float32, smallest / len(pieces), largest / len(pieces))
        return jnp.repeat(jnp.exp(heights), shape[axis_at] // shards_of).reshape((-1,) + (1,) * (len(shape) - axis_at - 1))

    factor_of = one(*pieces[0])
    for cut in pieces[1:]:
        factor_of = factor_of * one(*cut)
    return factor_of


def scatter_about(own_key, extent, spread, limit, cuts=(), kind=jnp.bfloat16):
    array = jax.random.normal(own_key, extent, jnp.float32) * spread
    if len(cuts) > 0:
        array = levels(own_key, extent, cuts, -0.22, 0.18) * array
    return jnp.clip(array, min=-limit, max=limit).astype(kind)


def setup_inputs(seed: int = 0) -> dict:
    arg_keys = jax.random.split(jax.random.key(seed), 9)
    activations = draw_activations(jax.random.fold_in(arg_keys[8], 71), 0)
    out_grad = draw_out_grad(jax.random.fold_in(arg_keys[8], 71), 0)
    basis = scatter_about(arg_keys[2], (LAYERS, D, RANK), D ** -0.5, 0.125, ((0, 4), (1, 2)), jnp.float32)
    first_moment = scatter_about(arg_keys[3], (LAYERS, RANK, FF), 1.0, 6.0, ((0, 4), (1, 2), (2, 4)), jnp.float32)
    second_moment = jnp.clip(jnp.exp(math.log(2.0) - 1.3862944 * jax.random.uniform(arg_keys[4], (LAYERS, RANK, FF), jnp.float32) ** levels(arg_keys[4], (LAYERS, RANK, FF), ((0, 4), (1, 2), (2, 4)), -0.2, 0.2)), 0.5, 2.0)
    gain_partial = scatter_about(arg_keys[5], (LAYERS, N_SHARD, D), 700.0, 4096.0, ((0, 4), (1, 2)), jnp.float32)
    gain_first = scatter_about(arg_keys[6], (LAYERS, D), 1.0, 6.0, ((0, 4), (1, 2)), jnp.float32)
    gain_second = jnp.clip(jnp.exp(math.log(2.0) - 1.3862944 * jax.random.uniform(arg_keys[7], (LAYERS, D), jnp.float32) ** levels(arg_keys[7], (LAYERS, D), ((0, 4), (1, 2)), -0.2, 0.2)), 0.5, 2.0)
    return {"activations": activations, "out_grad": out_grad, "basis": basis, "first_moment": first_moment, "second_moment": second_moment, "gain_partial": gain_partial, "gain_first": gain_first, "gain_second": gain_second}


exact_mode = lax.Precision.HIGHEST
beta_one = 0.9
beta_two = 0.999
adam_eps = 1e-08
clip_eps = 1e-06
ns_eps = 1e-07
coef_first = 3.4445
coef_second = -4.775
coef_third = 2.0315

def summed_gradient(tokens_in, grads_out):
    token_blocks = tokens_in.reshape(N_SHARD, TOK_DEV, D)
    grad_blocks = grads_out.reshape(N_SHARD, TOK_DEV, FF)

    def accumulate(total, pair):
        partial_grad = jnp.dot(pair[0].T, pair[1], preferred_element_type=jnp.float32)
        return (total + partial_grad, None)
    total, unused = lax.scan(accumulate, jnp.zeros((D, FF), jnp.float32), (token_blocks, grad_blocks))
    return total

def adam_direction(clipped, first_old, second_old):
    first_new = beta_one * first_old + (1.0 - beta_one) * clipped
    second_new = beta_two * second_old + (1.0 - beta_two) * clipped * clipped
    direction = first_new / (1.0 - beta_one ** STEP) / (jnp.sqrt(second_new / (1.0 - beta_two ** STEP)) + adam_eps)
    return (first_new, second_new, direction)

def orthogonalize(refreshed):
    current = refreshed / jnp.sqrt(jnp.sum(refreshed * refreshed) + ns_eps)
    for step_index in range(NS_STEPS):
        gram = jnp.dot(current.T, current, precision=exact_mode)
        mixer = coef_second * gram + coef_third * jnp.dot(gram, gram, precision=exact_mode)
        current = coef_first * current + jnp.dot(current, mixer, precision=exact_mode)
    return current

def reference(activations, out_grad, basis, first_moment, second_moment, gain_partial, gain_first, gain_second):
    grads = []
    square_sum = jnp.zeros((), jnp.float32)
    for layer_index in range(LAYERS):
        grad_layer = summed_gradient(activations[layer_index], out_grad[layer_index])
        grads.append(grad_layer)
        square_sum = square_sum + jnp.sum(grad_layer * grad_layer)
    gain_total = lax.optimization_barrier(jnp.sum(gain_partial, axis=1))
    square_sum = square_sum + jnp.sum(gain_total * gain_total)
    mean_sq = square_sum / float(LAYERS * (D * FF + D))
    clip = jnp.minimum(1.0, lax.rsqrt(mean_sq + clip_eps))
    updates = []
    firsts = []
    seconds = []
    bases = []
    for layer_index in range(LAYERS):
        proj = jnp.dot(basis[layer_index].T, grads[layer_index], precision=exact_mode)
        first_new, second_new, direction = adam_direction(clip * proj, first_moment[layer_index], second_moment[layer_index])
        updates.append(jnp.dot(basis[layer_index], direction, precision=exact_mode))
        firsts.append(first_new)
        seconds.append(second_new)
        refreshed = jnp.dot(grads[layer_index], proj.T, precision=exact_mode)
        bases.append(orthogonalize(refreshed))
    gain_first_new, gain_second_new, gain_dir = adam_direction(clip * gain_total, gain_first, gain_second)
    return (jnp.stack(updates), jnp.stack(firsts), jnp.stack(seconds), jnp.stack(bases), gain_dir, gain_first_new, gain_second_new)
```

```python
import jax
import jax.numpy as jnp
from jax import lax
from jax.sharding import PartitionSpec as P

D = 2048
FF = 8192
NS_STEPS = 5
STEP = 8


exact_mode = lax.Precision.HIGHEST
beta_one = 0.9
beta_two = 0.999
adam_eps = 1e-08
clip_eps = 1e-06
ns_eps = 1e-07
coef_first = 3.4445
coef_second = -4.775
coef_third = 2.0315


def adam_direction(clipped, first_old, second_old):
    first_new = beta_one * first_old + (1.0 - beta_one) * clipped
    second_new = beta_two * second_old + (1.0 - beta_two) * clipped * clipped
    direction = (
        first_new
        / (1.0 - beta_one**STEP)
        / (jnp.sqrt(second_new / (1.0 - beta_two**STEP)) + adam_eps)
    )
    return (first_new, second_new, direction)


def exact_dot(left, right):
    return jnp.dot(left, right, precision=exact_mode)


def ns_mixer(raw_gram):
    size = raw_gram.shape[0]
    same = lax.broadcasted_iota(jnp.int32, (size, size), 0) == lax.broadcasted_iota(
        jnp.int32, (size, size), 1
    )
    frob = jnp.sum(jnp.where(same, raw_gram, 0.0))
    gram = raw_gram / (frob + ns_eps)
    total = None
    for step_index in range(NS_STEPS):
        mixer = coef_second * gram + coef_third * exact_dot(gram, gram)
        mixer = mixer + jnp.where(same, coef_first, 0.0)
        total = mixer if total is None else exact_dot(total, mixer)
        if step_index + 1 < NS_STEPS:
            gram = exact_dot(mixer, exact_dot(gram, mixer))
    return total, lax.rsqrt(frob + ns_eps)


def shards(
    activations, out_grad, basis, first_moment, second_moment, gain_partial, gain_first, gain_second
):
    tensors = lax.axis_size("tensor")
    shard_pos = lax.axis_index("shard")
    layer_count = activations.shape[0]
    rows_here = basis.shape[1]
    rank_rows = first_moment.shape[1]
    cols_here = out_grad.shape[2]
    layer_index = 0
    tokens_in = activations[layer_index]
    grads_out = out_grad[layer_index]
    basis_here = basis[layer_index]

    def row_term(start, count, tokens_in=tokens_in, grads_out=grads_out):
        return lax.dot_general(
            tokens_in, grads_out, (((0,), (0,)), ((), ())), preferred_element_type=jnp.float32
        )

    grad_block = lax.psum_scatter(
        row_term(jnp.int32(0), lax.axis_size("shard") * rows_here),
        "shard",
        scatter_dimension=0,
        tiled=True,
    )
    part_proj = jnp.dot(basis_here.T, grad_block, precision=exact_mode)
    proj_full, gain_total = lax.psum((part_proj, gain_partial[layer_index, 0]), "shard")
    proj_rows = lax.dynamic_slice_in_dim(proj_full, shard_pos * rank_rows, rank_rows, 0)
    square_sum = jnp.sum(grad_block * grad_block)

    def refresh_term(start, count, grad_block=grad_block, proj_full=proj_full):
        return lax.dot_general(
            grad_block, proj_full, (((1,), (1,)), ((), ())), precision=exact_mode
        )

    refreshed = lax.psum_scatter(
        refresh_term(jnp.int32(0), lax.axis_size("tensor") * (rows_here // tensors)),
        "tensor",
        scatter_dimension=0,
        tiled=True,
    )
    kept_list = [basis_here]
    gain_own = lax.dynamic_slice_in_dim(gain_total, shard_pos * rows_here, rows_here, 0)
    square_sum = square_sum + jnp.sum(gain_own * gain_own) / float(tensors)
    proj_list = [proj_rows]
    gain_list = [gain_own]
    refresh_list = [refreshed]
    total_sq = lax.psum(square_sum, ("shard", "tensor", "section"))
    entry_count = float(lax.axis_size("section") * layer_count * (D * FF + D))
    clip = jnp.minimum(1.0, lax.rsqrt(total_sq / entry_count + clip_eps))
    layer_index = 0
    first_new, second_new, direction = adam_direction(
        clip * proj_list[layer_index], first_moment[layer_index], second_moment[layer_index]
    )
    firsts = [first_new]
    seconds = [second_new]
    kept_basis = kept_list[layer_index]

    def fold_rows(total, piece, start, kept_basis=kept_basis):
        return jnp.dot(kept_basis, piece, precision=exact_mode)

    empty = jnp.zeros((rows_here, cols_here), jnp.float32)
    update_here = fold_rows(
        empty, lax.all_gather(direction, "shard", axis=0, tiled=True), jnp.int32(0)
    )
    updates = [update_here]
    refreshed = refresh_list[layer_index]
    raw_gram = lax.psum(
        jnp.dot(refreshed.T, refreshed, precision=exact_mode), ("shard", "tensor")
    )
    mixer, scale = ns_mixer(raw_gram)
    current = exact_dot(refreshed * scale, mixer)
    bases = [current]
    gain_first_new, gain_second_new, gain_dir = adam_direction(
        clip * gain_list[layer_index], gain_first[layer_index], gain_second[layer_index]
    )
    gain_steps = [gain_dir]
    gain_firsts = [gain_first_new]
    gain_seconds = [gain_second_new]
    return (
        jnp.stack(updates),
        jnp.stack(firsts),
        jnp.stack(seconds),
        jnp.stack(bases),
        jnp.stack(gain_steps),
        jnp.stack(gain_firsts),
        jnp.stack(gain_seconds),
    )


def solution(mesh):
    placed = (
        P("section", "shard", None),
        P("section", "shard", "tensor"),
        P("section", "shard", None),
        P("section", "shard", "tensor"),
        P("section", "shard", "tensor"),
        P("section", "shard", None),
        P("section", "shard"),
        P("section", "shard"),
    )
    return jax.shard_map(
        shards,
        mesh=mesh,
        in_specs=placed,
        out_specs=(
            P("section", "shard", "tensor"),
            P("section", "shard", "tensor"),
            P("section", "shard", "tensor"),
            P("section", ("shard", "tensor"), None),
            P("section", "shard"),
            P("section", "shard"),
            P("section", "shard"),
        ),
        check_vma=False,
    )
```

```python
import functools

import jax
import jax.numpy as jnp
from jax import lax
from jax.sharding import PartitionSpec as P
from jax.experimental import pallas as pl
from jax.experimental.pallas import tpu as pltpu

D = 2048
FF = 8192
LAYERS = 4
NS_STEPS = 5
STEP = 8


exact_mode = lax.Precision.HIGHEST
beta_one = 0.9
beta_two = 0.999
adam_eps = 1e-08
clip_eps = 1e-06
ns_eps = 1e-07
coef_first = 3.4445
coef_second = -4.775
coef_third = 2.0315


def adam_direction(clipped, first_old, second_old):
    first_new = beta_one * first_old + (1.0 - beta_one) * clipped
    second_new = beta_two * second_old + (1.0 - beta_two) * clipped * clipped
    direction = (
        first_new
        / (1.0 - beta_one**STEP)
        / (jnp.sqrt(second_new / (1.0 - beta_two**STEP)) + adam_eps)
    )
    return (first_new, second_new, direction)


def exact_dot(left, right):
    return jnp.dot(left, right, precision=exact_mode)


def ns_mixer(raw_gram):
    size = raw_gram.shape[0]
    same = lax.broadcasted_iota(jnp.int32, (size, size), 0) == lax.broadcasted_iota(
        jnp.int32, (size, size), 1
    )
    frob = jnp.sum(jnp.where(same, raw_gram, 0.0))
    gram = raw_gram / (frob + ns_eps)
    total = None
    for step_index in range(NS_STEPS):
        mixer = coef_second * gram + coef_third * exact_dot(gram, gram)
        mixer = mixer + jnp.where(same, coef_first, 0.0)
        total = mixer if total is None else exact_dot(total, mixer)
        if step_index + 1 < NS_STEPS:
            gram = exact_dot(mixer, exact_dot(gram, mixer))
    return total, lax.rsqrt(frob + ns_eps)


def shards(
    activations, out_grad, basis, first_moment, second_moment, gain_partial, gain_first, gain_second
):
    tensors = lax.axis_size("tensor")
    shard_pos = lax.axis_index("shard")
    layer_count = activations.shape[0]
    rows_here = basis.shape[1]
    rank_rows = first_moment.shape[1]
    cols_here = out_grad.shape[2]
    layer_index = 0
    tokens_in = activations[layer_index]
    grads_out = out_grad[layer_index]
    basis_here = basis[layer_index]

    def row_term(start, count, tokens_in=tokens_in, grads_out=grads_out):
        return lax.dot_general(
            tokens_in, grads_out, (((0,), (0,)), ((), ())), preferred_element_type=jnp.float32
        )

    grad_block = lax.psum_scatter(
        row_term(jnp.int32(0), lax.axis_size("shard") * rows_here),
        "shard",
        scatter_dimension=0,
        tiled=True,
    )
    part_proj = jnp.dot(basis_here.T, grad_block, precision=exact_mode)
    proj_full, gain_total = lax.psum((part_proj, gain_partial[layer_index, 0]), "shard")
    proj_rows = lax.dynamic_slice_in_dim(proj_full, shard_pos * rank_rows, rank_rows, 0)
    square_sum = jnp.sum(grad_block * grad_block)

    def refresh_term(start, count, grad_block=grad_block, proj_full=proj_full):
        return lax.dot_general(
            grad_block, proj_full, (((1,), (1,)), ((), ())), precision=exact_mode
        )

    refreshed = lax.psum_scatter(
        refresh_term(jnp.int32(0), lax.axis_size("tensor") * (rows_here // tensors)),
        "tensor",
        scatter_dimension=0,
        tiled=True,
    )
    kept_list = [basis_here]
    gain_own = lax.dynamic_slice_in_dim(gain_total, shard_pos * rows_here, rows_here, 0)
    square_sum = square_sum + jnp.sum(gain_own * gain_own) / float(tensors)
    proj_list = [proj_rows]
    gain_list = [gain_own]
    refresh_list = [refreshed]
    total_sq = lax.psum(square_sum, ("shard", "tensor", "section"))
    entry_count = float(lax.axis_size("section") * layer_count * (D * FF + D))
    clip = jnp.minimum(1.0, lax.rsqrt(total_sq / entry_count + clip_eps))
    layer_index = 0
    first_new, second_new, direction = adam_direction(
        clip * proj_list[layer_index], first_moment[layer_index], second_moment[layer_index]
    )
    firsts = [first_new]
    seconds = [second_new]
    kept_basis = kept_list[layer_index]

    def fold_rows(total, piece, start, kept_basis=kept_basis):
        return jnp.dot(kept_basis, piece, precision=exact_mode)

    empty = jnp.zeros((rows_here, cols_here), jnp.float32)
    update_here = fold_rows(
        empty, lax.all_gather(direction, "shard", axis=0, tiled=True), jnp.int32(0)
    )
    updates = [update_here]
    refreshed = refresh_list[layer_index]
    raw_gram = lax.psum(
        jnp.dot(refreshed.T, refreshed, precision=exact_mode), ("shard", "tensor")
    )
    mixer, scale = ns_mixer(raw_gram)
    current = exact_dot(refreshed * scale, mixer)
    bases = [current]
    gain_first_new, gain_second_new, gain_dir = adam_direction(
        clip * gain_list[layer_index], gain_first[layer_index], gain_second[layer_index]
    )
    gain_steps = [gain_dir]
    gain_firsts = [gain_first_new]
    gain_seconds = [gain_second_new]
    return (
        jnp.stack(updates),
        jnp.stack(firsts),
        jnp.stack(seconds),
        jnp.stack(bases),
        jnp.stack(gain_steps),
        jnp.stack(gain_firsts),
        jnp.stack(gain_seconds),
    )


MESH = pl.DeviceIdType.MESH
CHUNK = 256
BLOCK = 256


def exact_dims(left, right, dims):
    return lax.dot_general(
        left, right, (dims, ((), ())), precision=exact_mode, preferred_element_type=jnp.float32
    )


def exchange_kernel(
    tokens_ref,
    grads_ref,
    basis_t_ref,
    gain_ref,
    proj_ref,
    rows_ref,
    square_ref,
    gain_out_ref,
    sent,
    landed,
    own,
    part,
    part_landed,
    gain_landed,
    grad_send,
    grad_recv,
    part_send,
    part_recv,
    gain_send,
    gain_recv,
):
    chunks, rows_here, width = own.shape
    me = lax.axis_index("shard")
    other = 1 - me
    barrier = pltpu.get_barrier_semaphore()
    pl.semaphore_signal(barrier, inc=1, device_id={"shard": other}, device_id_type=MESH)
    pl.semaphore_wait(barrier, 1)

    def remote(source, target, send, recv):
        return pltpu.make_async_remote_copy(
            src_ref=source,
            dst_ref=target,
            send_sem=send,
            recv_sem=recv,
            device_id={"shard": other},
            device_id_type=MESH,
        )

    def grad_copy(c):
        return remote(sent.at[c], landed.at[c], grad_send.at[c], grad_recv.at[c])

    def part_copy(c):
        return remote(part.at[c], part_landed.at[c], part_send.at[c], part_recv.at[c])

    gain_copy = remote(gain_ref, gain_landed, gain_send, gain_recv)
    gain_copy.start()

    def multiply(target, half, c):
        columns = pl.ds(pl.multiple_of(c * width, width), width)

        @pl.loop(0, rows_here // BLOCK)
        def _(m):
            start = pl.multiple_of(half * rows_here + m * BLOCK, BLOCK)
            target[c, pl.ds(pl.multiple_of(m * BLOCK, BLOCK), BLOCK), :] = lax.dot_general(
                tokens_ref[:, pl.ds(start, BLOCK)],
                grads_ref[:, columns],
                (((0,), (0,)), ((), ())),
                preferred_element_type=jnp.float32,
            )

    @pl.loop(0, chunks)
    def _(c):
        multiply(sent, other, c)
        grad_copy(c).start()

    @pl.loop(0, chunks)
    def _(c):
        multiply(own, me, c)

    rows_ref[...] = jnp.zeros_like(rows_ref)
    square_ref[...] = jnp.zeros_like(square_ref)

    def refresh(c):
        part_copy(c).wait_recv()
        proj = part[c] + part_landed[c]
        proj_ref[c] = proj

        @pl.loop(0, rows_here // BLOCK)
        def _(m):
            block = pl.ds(pl.multiple_of(m * BLOCK, BLOCK), BLOCK)
            rows_ref[block, :] += exact_dims(own[c, block, :], proj, ((1,), (1,)))

    lag = min(4, chunks)

    @pl.loop(0, chunks)
    def _(c):
        grad_copy(c).wait_recv()

        @pl.loop(0, rows_here // BLOCK)
        def _(m):
            block = pl.ds(pl.multiple_of(m * BLOCK, BLOCK), BLOCK)
            total = own[c, block, :] + landed[c, block, :]
            own[c, block, :] = total
            square_ref[...] += jnp.sum((total * total).reshape(BLOCK // 8, 8, width), axis=0)

        part[c] = exact_dims(basis_t_ref[...], own[c], ((1,), (0,)))
        part_copy(c).start()

        @pl.when(c >= lag)
        def _():
            refresh(c - lag)

    @pl.loop(chunks - lag, chunks)
    def _(c):
        refresh(c)

    gain_copy.wait_recv()
    gain_out_ref[...] = gain_ref[...] + gain_landed[...]
    gain_copy.wait_send()

    @pl.loop(0, chunks)
    def _(c):
        grad_copy(c).wait_send()
        part_copy(c).wait_send()


def exchange(tokens_in, grads_out, basis_t, gain):
    rank, rows_here = basis_t.shape
    cols = grads_out.shape[1]
    chunks = cols // CHUNK
    vmem = pl.BlockSpec(memory_space=pltpu.VMEM)
    f32 = jnp.float32
    flops = 2 * tokens_in.shape[0] * tokens_in.shape[1] * cols + 24 * rank * rows_here * cols
    return pl.pallas_call(
        exchange_kernel,
        out_shape=(
            jax.ShapeDtypeStruct((chunks, rank, CHUNK), f32),
            jax.ShapeDtypeStruct((rows_here, rank), f32),
            jax.ShapeDtypeStruct((8, CHUNK), f32),
            jax.ShapeDtypeStruct(gain.shape, f32),
        ),
        in_specs=[vmem] * 4,
        out_specs=(vmem,) * 4,
        scratch_shapes=[
            pltpu.VMEM((chunks, rows_here, CHUNK), f32),
            pltpu.VMEM((chunks, rows_here, CHUNK), f32),
            pltpu.VMEM((chunks, rows_here, CHUNK), f32),
            pltpu.VMEM((chunks, rank, CHUNK), f32),
            pltpu.VMEM((chunks, rank, CHUNK), f32),
            pltpu.VMEM(gain.shape, f32),
            pltpu.SemaphoreType.DMA((chunks,)),
            pltpu.SemaphoreType.DMA((chunks,)),
            pltpu.SemaphoreType.DMA((chunks,)),
            pltpu.SemaphoreType.DMA((chunks,)),
            pltpu.SemaphoreType.DMA,
            pltpu.SemaphoreType.DMA,
        ],
        compiler_params=pltpu.CompilerParams(
            collective_id=0, has_side_effects=True, vmem_limit_bytes=60 * 2**20
        ),
        cost_estimate=pl.CostEstimate(flops=flops, bytes_accessed=2**25, transcendentals=0),
        name="exchange",
    )(tokens_in, grads_out, basis_t, gain)


def finish_kernel(
    axes,
    proj_ref,
    rows_ref,
    square_ref,
    gain_ref,
    first_ref,
    second_ref,
    gain_first_ref,
    gain_second_ref,
    first_out,
    second_out,
    direction_out,
    basis_out,
    gain_step_out,
    gain_first_out,
    gain_second_out,
    row_slots,
    one_square,
    section_slots,
    group_square,
    group_slots,
    dir_own,
    dir_landed,
    gram,
    gram_slots,
    gram_part,
    gram_full,
    row_sems,
    section_sems,
    group_sems,
    dir_sems,
    gram_sems,
    full_sems,
):
    shards_n, tensors_n, sections_n, entry_count = axes
    group_n = shards_n * tensors_n
    chunks, rank, width = proj_ref.shape
    rank_rows = rank // shards_n
    shard_pos = lax.axis_index("shard")
    tensor_pos = lax.axis_index("tensor")
    section_pos = lax.axis_index("section")
    me = shard_pos * tensors_n + tensor_pos
    piece = rank // group_n

    def in_group(step):
        peer = lax.rem(me + step, group_n)
        return peer, {"shard": peer // tensors_n, "tensor": lax.rem(peer, tensors_n)}

    def in_section(step):
        return {"section": lax.rem(section_pos + step, sections_n)}

    barrier = pltpu.get_barrier_semaphore()
    for step in range(1, group_n):
        pl.semaphore_signal(barrier, inc=1, device_id=in_group(step)[1], device_id_type=MESH)
    for step in range(1, sections_n):
        pl.semaphore_signal(barrier, inc=1, device_id=in_section(step), device_id_type=MESH)
    pl.semaphore_wait(barrier, group_n - 1 + sections_n - 1)

    def remote(source, target, sems, k, where):
        return pltpu.make_async_remote_copy(
            src_ref=source,
            dst_ref=target,
            send_sem=sems.at[0, k],
            recv_sem=sems.at[1, k],
            device_id=where,
            device_id_type=MESH,
        )

    gain_squares = gain_ref[...] * gain_ref[...]
    share = jnp.sum(gain_squares) / float(group_n)
    local = jnp.sum(square_ref[...]) + share
    one_square[...] = jnp.full(one_square.shape, local, jnp.float32)
    section_copies = []
    for step in range(1, sections_n):
        copy = remote(
            one_square, section_slots.at[section_pos], section_sems, step, in_section(step)
        )
        copy.start()
        section_copies.append(copy)
    section_slots[section_pos] = one_square[...]

    row_copies = []
    for step in range(1, tensors_n):
        peer = lax.rem(tensor_pos + step, tensors_n)
        copy = remote(rows_ref.at[peer], row_slots.at[step], row_sems, step, {"tensor": peer})
        copy.start()
        row_copies.append(copy)

    for copy in section_copies:
        copy.wait_recv()
    total = section_slots[0]
    for k in range(1, sections_n):
        total = total + section_slots[k]
    group_square[...] = total
    group_copies = []
    for step in range(1, group_n):
        copy = remote(
            group_square, group_slots.at[me], group_sems, step, in_group(step)[1]
        )
        copy.start()
        group_copies.append(copy)
    group_slots[me] = group_square[...]
    for copy in group_copies:
        copy.wait_recv()
    total = group_slots[0]
    for k in range(1, group_n):
        total = total + group_slots[k]
    clip_tile = jnp.minimum(1.0, lax.rsqrt(total / entry_count + clip_eps))
    clip = clip_tile[0:1, 0:1]

    def dir_copy(c):
        columns = pl.ds(pl.multiple_of(c * width, width), width)
        return remote(
            dir_own.at[:, columns],
            dir_landed.at[:, columns],
            dir_sems,
            c,
            {"shard": 1 - shard_pos},
        )

    @pl.loop(0, chunks)
    def _(c):
        columns = pl.ds(pl.multiple_of(c * width, width), width)
        rows = pl.ds(pl.multiple_of(shard_pos * rank_rows, rank_rows), rank_rows)
        first_new, second_new, direction = adam_direction(
            clip * proj_ref[c, rows, :], first_ref[:, columns], second_ref[:, columns]
        )
        first_out[:, columns] = first_new
        second_out[:, columns] = second_new
        dir_own[:, columns] = direction
        dir_copy(c).start()

    first_new, second_new, direction = adam_direction(
        clip * gain_ref[shard_pos], gain_first_ref[...], gain_second_ref[...]
    )
    gain_first_out[...] = first_new
    gain_second_out[...] = second_new
    gain_step_out[...] = direction

    for copy in row_copies:
        copy.wait_recv()
    current = rows_ref[tensor_pos]
    for step in range(1, tensors_n):
        current = current + row_slots[step]
    gram[...] = exact_dims(current, current, ((0,), (0,)))
    gram_copies = []
    for step in range(1, group_n):
        peer, where = in_group(step)
        copy = remote(
            gram.at[pl.ds(pl.multiple_of(peer * piece, piece), piece), :],
            gram_slots.at[step],
            gram_sems,
            step,
            where,
        )
        copy.start()
        gram_copies.append(copy)
    mine = pl.ds(pl.multiple_of(me * piece, piece), piece)
    summed = gram[mine, :]
    for step, copy in enumerate(gram_copies):
        copy.wait_recv()
        summed = summed + gram_slots[step + 1]
    gram_part[...] = summed
    full_copies = []
    for step in range(1, group_n):
        copy = remote(gram_part, gram_full.at[mine, :], full_sems, step, in_group(step)[1])
        copy.start()
        full_copies.append(copy)
    gram_full[mine, :] = summed
    for copy in full_copies:
        copy.wait_recv()
    mixer, scale = ns_mixer(gram_full[...])
    basis_out[...] = exact_dot(current * scale, mixer)

    @pl.loop(0, chunks)
    def _(c):
        dir_copy(c).wait_recv()
        dir_copy(c).wait_send()

    direction_out[shard_pos] = dir_own[...]
    direction_out[1 - shard_pos] = dir_landed[...]
    for copies in (section_copies, row_copies, group_copies, gram_copies, full_copies):
        for copy in copies:
            copy.wait_send()


def finish(axes, proj, rows, square, gain, first, second, gain_first, gain_second):
    shards_n, tensors_n, sections_n, _ = axes
    group_n = shards_n * tensors_n
    chunks, rank, width = proj.shape
    rank_rows, cols = first.shape
    f32 = jnp.float32
    vmem = pl.BlockSpec(memory_space=pltpu.VMEM)
    shape = jax.ShapeDtypeStruct
    tile = (8, 128)
    dma = pltpu.SemaphoreType.DMA
    return pl.pallas_call(
        functools.partial(finish_kernel, axes),
        out_shape=(
            shape((rank_rows, cols), f32),
            shape((rank_rows, cols), f32),
            shape((shards_n, rank_rows, cols), f32),
            shape((rank, rank), f32),
            shape(gain_first.shape, f32),
            shape(gain_first.shape, f32),
            shape(gain_first.shape, f32),
        ),
        in_specs=[vmem] * 8,
        out_specs=(vmem,) * 7,
        scratch_shapes=[
            pltpu.VMEM(rows.shape, f32),
            pltpu.VMEM(tile, f32),
            pltpu.VMEM((sections_n,) + tile, f32),
            pltpu.VMEM(tile, f32),
            pltpu.VMEM((group_n,) + tile, f32),
            pltpu.VMEM((rank_rows, cols), f32),
            pltpu.VMEM((rank_rows, cols), f32),
            pltpu.VMEM((rank, rank), f32),
            pltpu.VMEM((group_n, rank // group_n, rank), f32),
            pltpu.VMEM((rank // group_n, rank), f32),
            pltpu.VMEM((rank, rank), f32),
            dma((2, tensors_n)),
            dma((2, sections_n)),
            dma((2, group_n)),
            dma((2, chunks)),
            dma((2, group_n)),
            dma((2, group_n)),
        ],
        compiler_params=pltpu.CompilerParams(
            collective_id=1, has_side_effects=True, vmem_limit_bytes=48 * 2**20
        ),
        cost_estimate=pl.CostEstimate(flops=2**32, bytes_accessed=2**24, transcendentals=2**20),
        name="finish",
    )(proj, rows, square, gain, first, second, gain_first, gain_second)


def paired(
    activations, out_grad, basis, first_moment, second_moment, gain_partial, gain_first, gain_second
):
    shards_n = lax.axis_size("shard")
    tensors_n = lax.axis_size("tensor")
    sections_n = lax.axis_size("section")
    rows_here = basis.shape[1]
    rank = basis.shape[2]
    cols = out_grad.shape[2]
    basis_here = basis[0]
    gain = gain_partial[0, 0].reshape(shards_n, 8, rows_here // 8)
    proj, rows, square, gain_total = exchange(activations[0], out_grad[0], basis_here.T, gain)
    axes = (shards_n, tensors_n, sections_n, float(sections_n * (D * FF + D)))
    gain_shape = (8, rows_here // 8)
    first, second, direction, new_basis, gain_step, gain_first_new, gain_second_new = finish(
        axes,
        proj,
        rows.reshape(tensors_n, rows_here // tensors_n, rank),
        square,
        gain_total,
        first_moment[0],
        second_moment[0],
        gain_first[0].reshape(gain_shape),
        gain_second[0].reshape(gain_shape),
    )
    update = exact_dot(basis_here, direction.reshape(rank, cols))
    return (
        update[None],
        first[None],
        second[None],
        new_basis[None],
        gain_step.reshape(1, rows_here),
        gain_first_new.reshape(1, rows_here),
        gain_second_new.reshape(1, rows_here),
    )


def solution(mesh):
    placed = (
        P("section", "shard", None),
        P("section", "shard", "tensor"),
        P("section", "shard", None),
        P("section", "shard", "tensor"),
        P("section", "shard", "tensor"),
        P("section", "shard", None),
        P("section", "shard"),
        P("section", "shard"),
    )
    one_layer = mesh.shape["section"] == LAYERS
    body = paired if mesh.shape["shard"] == 2 and one_layer else shards
    return jax.shard_map(
        body,
        mesh=mesh,
        in_specs=placed,
        out_specs=(
            P("section", "shard", "tensor"),
            P("section", "shard", "tensor"),
            P("section", "shard", "tensor"),
            P("section", ("shard", "tensor"), None),
            P("section", "shard"),
            P("section", "shard"),
            P("section", "shard"),
        ),
        check_vma=False,
    )
```

```python
import functools

import jax
import jax.numpy as jnp
from jax import lax
from jax.sharding import PartitionSpec as P
from jax.experimental import pallas as pl
from jax.experimental.pallas import tpu as pltpu

D = 2048
FF = 8192
LAYERS = 4
NS_STEPS = 5
STEP = 8


exact_mode = lax.Precision.HIGHEST
beta_one = 0.9
beta_two = 0.999
adam_eps = 1e-08
clip_eps = 1e-06
ns_eps = 1e-07
coef_first = 3.4445
coef_second = -4.775
coef_third = 2.0315


def adam_direction(clipped, first_old, second_old):
    first_new = beta_one * first_old + (1.0 - beta_one) * clipped
    second_new = beta_two * second_old + (1.0 - beta_two) * clipped * clipped
    direction = (
        first_new
        / (1.0 - beta_one**STEP)
        / (jnp.sqrt(second_new / (1.0 - beta_two**STEP)) + adam_eps)
    )
    return (first_new, second_new, direction)


def exact_dot(left, right):
    return jnp.dot(left, right, precision=exact_mode)


def ns_mixer(raw_gram):
    size = raw_gram.shape[0]
    same = lax.broadcasted_iota(jnp.int32, (size, size), 0) == lax.broadcasted_iota(
        jnp.int32, (size, size), 1
    )
    frob = jnp.sum(jnp.where(same, raw_gram, 0.0))
    gram = raw_gram / (frob + ns_eps)
    total = None
    for step_index in range(NS_STEPS):
        mixer = coef_second * gram + coef_third * exact_dot(gram, gram)
        mixer = mixer + jnp.where(same, coef_first, 0.0)
        total = mixer if total is None else exact_dot(total, mixer)
        if step_index + 1 < NS_STEPS:
            gram = exact_dot(mixer, exact_dot(gram, mixer))
    return total, lax.rsqrt(frob + ns_eps)


def shards(
    activations, out_grad, basis, first_moment, second_moment, gain_partial, gain_first, gain_second
):
    tensors = lax.axis_size("tensor")
    shard_pos = lax.axis_index("shard")
    layer_count = activations.shape[0]
    rows_here = basis.shape[1]
    rank_rows = first_moment.shape[1]
    cols_here = out_grad.shape[2]
    layer_index = 0
    tokens_in = activations[layer_index]
    grads_out = out_grad[layer_index]
    basis_here = basis[layer_index]

    def row_term(start, count, tokens_in=tokens_in, grads_out=grads_out):
        return lax.dot_general(
            tokens_in, grads_out, (((0,), (0,)), ((), ())), preferred_element_type=jnp.float32
        )

    grad_block = lax.psum_scatter(
        row_term(jnp.int32(0), lax.axis_size("shard") * rows_here),
        "shard",
        scatter_dimension=0,
        tiled=True,
    )
    part_proj = jnp.dot(basis_here.T, grad_block, precision=exact_mode)
    proj_full, gain_total = lax.psum((part_proj, gain_partial[layer_index, 0]), "shard")
    proj_rows = lax.dynamic_slice_in_dim(proj_full, shard_pos * rank_rows, rank_rows, 0)
    square_sum = jnp.sum(grad_block * grad_block)

    def refresh_term(start, count, grad_block=grad_block, proj_full=proj_full):
        return lax.dot_general(
            grad_block, proj_full, (((1,), (1,)), ((), ())), precision=exact_mode
        )

    refreshed = lax.psum_scatter(
        refresh_term(jnp.int32(0), lax.axis_size("tensor") * (rows_here // tensors)),
        "tensor",
        scatter_dimension=0,
        tiled=True,
    )
    kept_list = [basis_here]
    gain_own = lax.dynamic_slice_in_dim(gain_total, shard_pos * rows_here, rows_here, 0)
    square_sum = square_sum + jnp.sum(gain_own * gain_own) / float(tensors)
    proj_list = [proj_rows]
    gain_list = [gain_own]
    refresh_list = [refreshed]
    total_sq = lax.psum(square_sum, ("shard", "tensor", "section"))
    entry_count = float(lax.axis_size("section") * layer_count * (D * FF + D))
    clip = jnp.minimum(1.0, lax.rsqrt(total_sq / entry_count + clip_eps))
    layer_index = 0
    first_new, second_new, direction = adam_direction(
        clip * proj_list[layer_index], first_moment[layer_index], second_moment[layer_index]
    )
    firsts = [first_new]
    seconds = [second_new]
    kept_basis = kept_list[layer_index]

    def fold_rows(total, piece, start, kept_basis=kept_basis):
        return jnp.dot(kept_basis, piece, precision=exact_mode)

    empty = jnp.zeros((rows_here, cols_here), jnp.float32)
    update_here = fold_rows(
        empty, lax.all_gather(direction, "shard", axis=0, tiled=True), jnp.int32(0)
    )
    updates = [update_here]
    refreshed = refresh_list[layer_index]
    raw_gram = lax.psum(
        jnp.dot(refreshed.T, refreshed, precision=exact_mode), ("shard", "tensor")
    )
    mixer, scale = ns_mixer(raw_gram)
    current = exact_dot(refreshed * scale, mixer)
    bases = [current]
    gain_first_new, gain_second_new, gain_dir = adam_direction(
        clip * gain_list[layer_index], gain_first[layer_index], gain_second[layer_index]
    )
    gain_steps = [gain_dir]
    gain_firsts = [gain_first_new]
    gain_seconds = [gain_second_new]
    return (
        jnp.stack(updates),
        jnp.stack(firsts),
        jnp.stack(seconds),
        jnp.stack(bases),
        jnp.stack(gain_steps),
        jnp.stack(gain_firsts),
        jnp.stack(gain_seconds),
    )


MESH = pl.DeviceIdType.MESH
CHUNK = 256
BLOCK = 256


def exact_dims(left, right, dims):
    return lax.dot_general(
        left, right, (dims, ((), ())), precision=exact_mode, preferred_element_type=jnp.float32
    )


def exchange_kernel(
    tokens_hbm,
    grads_hbm,
    basis_t_ref,
    gain_ref,
    proj_ref,
    rows_ref,
    square_ref,
    gain_out_ref,
    tokens_ref,
    grads_ref,
    sent,
    landed,
    own,
    part,
    part_landed,
    gain_landed,
    grad_send,
    grad_recv,
    part_send,
    part_recv,
    gain_send,
    gain_recv,
    token_sems,
    column_sems,
):
    chunks, rows_here, width = own.shape
    me = lax.axis_index("shard")
    other = 1 - me

    def token_copy(half, k):
        rows = pl.ds(pl.multiple_of(half * rows_here, rows_here), rows_here)
        return pltpu.make_async_copy(
            tokens_hbm.at[:, rows], tokens_ref.at[:, rows], token_sems.at[k]
        )

    def column_copy(c):
        columns = pl.ds(pl.multiple_of(c * width, width), width)
        return pltpu.make_async_copy(
            grads_hbm.at[:, columns], grads_ref.at[:, columns], column_sems.at[c]
        )

    token_copy(other, 0).start()

    @pl.loop(0, chunks)
    def _(c):
        column_copy(c).start()

    token_copy(me, 1).start()
    barrier = pltpu.get_barrier_semaphore()
    pl.semaphore_signal(barrier, inc=1, device_id={"shard": other}, device_id_type=MESH)
    pl.semaphore_wait(barrier, 1)

    def remote(source, target, send, recv):
        return pltpu.make_async_remote_copy(
            src_ref=source,
            dst_ref=target,
            send_sem=send,
            recv_sem=recv,
            device_id={"shard": other},
            device_id_type=MESH,
        )

    def grad_copy(c):
        return remote(sent.at[c], landed.at[c], grad_send.at[c], grad_recv.at[c])

    def part_copy(c):
        return remote(part.at[c], part_landed.at[c], part_send.at[c], part_recv.at[c])

    gain_copy = remote(gain_ref, gain_landed, gain_send, gain_recv)
    gain_copy.start()

    def multiply(target, half, c):
        columns = pl.ds(pl.multiple_of(c * width, width), width)

        @pl.loop(0, rows_here // BLOCK)
        def _(m):
            start = pl.multiple_of(half * rows_here + m * BLOCK, BLOCK)
            target[c, pl.ds(pl.multiple_of(m * BLOCK, BLOCK), BLOCK), :] = lax.dot_general(
                tokens_ref[:, pl.ds(start, BLOCK)],
                grads_ref[:, columns],
                (((0,), (0,)), ((), ())),
                preferred_element_type=jnp.float32,
            )

    token_copy(other, 0).wait()

    @pl.loop(0, chunks)
    def _(c):
        column_copy(c).wait()
        multiply(sent, other, c)
        grad_copy(c).start()

    token_copy(me, 1).wait()

    @pl.loop(0, chunks)
    def _(c):
        multiply(own, me, c)

    rows_ref[...] = jnp.zeros_like(rows_ref)
    square_ref[...] = jnp.zeros_like(square_ref)

    def refresh(c):
        part_copy(c).wait_recv()
        proj = part[c] + part_landed[c]
        proj_ref[c] = proj

        @pl.loop(0, rows_here // BLOCK)
        def _(m):
            block = pl.ds(pl.multiple_of(m * BLOCK, BLOCK), BLOCK)
            rows_ref[block, :] += exact_dims(own[c, block, :], proj, ((1,), (1,)))

    lag = min(4, chunks)

    @pl.loop(0, chunks)
    def _(c):
        grad_copy(c).wait_recv()

        @pl.loop(0, rows_here // BLOCK)
        def _(m):
            block = pl.ds(pl.multiple_of(m * BLOCK, BLOCK), BLOCK)
            total = own[c, block, :] + landed[c, block, :]
            own[c, block, :] = total
            square_ref[...] += jnp.sum((total * total).reshape(BLOCK // 8, 8, width), axis=0)

        part[c] = exact_dims(basis_t_ref[...], own[c], ((1,), (0,)))
        part_copy(c).start()

        @pl.when(c >= lag)
        def _():
            refresh(c - lag)

    @pl.loop(chunks - lag, chunks)
    def _(c):
        refresh(c)

    gain_copy.wait_recv()
    gain_out_ref[...] = gain_ref[...] + gain_landed[...]
    gain_copy.wait_send()

    @pl.loop(0, chunks)
    def _(c):
        grad_copy(c).wait_send()
        part_copy(c).wait_send()


def exchange(tokens_in, grads_out, basis_t, gain):
    rank, rows_here = basis_t.shape
    cols = grads_out.shape[1]
    chunks = cols // CHUNK
    vmem = pl.BlockSpec(memory_space=pltpu.VMEM)
    f32 = jnp.float32
    flops = 2 * tokens_in.shape[0] * tokens_in.shape[1] * cols + 24 * rank * rows_here * cols
    return pl.pallas_call(
        exchange_kernel,
        out_shape=(
            jax.ShapeDtypeStruct((chunks, rank, CHUNK), f32),
            jax.ShapeDtypeStruct((rows_here, rank), f32),
            jax.ShapeDtypeStruct((8, CHUNK), f32),
            jax.ShapeDtypeStruct(gain.shape, f32),
        ),
        in_specs=[pl.BlockSpec(memory_space=pl.ANY)] * 2 + [vmem] * 2,
        out_specs=(vmem,) * 4,
        scratch_shapes=[
            pltpu.VMEM(tokens_in.shape, tokens_in.dtype),
            pltpu.VMEM(grads_out.shape, grads_out.dtype),
            pltpu.VMEM((chunks, rows_here, CHUNK), f32),
            pltpu.VMEM((chunks, rows_here, CHUNK), f32),
            pltpu.VMEM((chunks, rows_here, CHUNK), f32),
            pltpu.VMEM((chunks, rank, CHUNK), f32),
            pltpu.VMEM((chunks, rank, CHUNK), f32),
            pltpu.VMEM(gain.shape, f32),
            pltpu.SemaphoreType.DMA((chunks,)),
            pltpu.SemaphoreType.DMA((chunks,)),
            pltpu.SemaphoreType.DMA((chunks,)),
            pltpu.SemaphoreType.DMA((chunks,)),
            pltpu.SemaphoreType.DMA,
            pltpu.SemaphoreType.DMA,
            pltpu.SemaphoreType.DMA((2,)),
            pltpu.SemaphoreType.DMA((chunks,)),
        ],
        compiler_params=pltpu.CompilerParams(
            collective_id=0, has_side_effects=True, vmem_limit_bytes=60 * 2**20
        ),
        cost_estimate=pl.CostEstimate(flops=flops, bytes_accessed=2**25, transcendentals=0),
        name="exchange",
    )(tokens_in, grads_out, basis_t, gain)


def finish_kernel(
    axes,
    proj_ref,
    rows_ref,
    square_ref,
    gain_ref,
    first_hbm,
    second_hbm,
    gain_first_ref,
    gain_second_ref,
    first_out,
    second_out,
    direction_out,
    basis_out,
    gain_step_out,
    gain_first_out,
    gain_second_out,
    row_slots,
    one_square,
    section_slots,
    group_square,
    group_slots,
    dir_own,
    dir_landed,
    gram,
    gram_slots,
    gram_part,
    gram_full,
    row_sems,
    section_sems,
    group_sems,
    dir_sems,
    gram_sems,
    full_sems,
    first_ref,
    second_ref,
    moment_sems,
):
    shards_n, tensors_n, sections_n, entry_count = axes
    group_n = shards_n * tensors_n
    chunks, rank, width = proj_ref.shape
    rank_rows = rank // shards_n
    shard_pos = lax.axis_index("shard")
    tensor_pos = lax.axis_index("tensor")
    section_pos = lax.axis_index("section")
    me = shard_pos * tensors_n + tensor_pos
    piece = rank // group_n
    first_copy = pltpu.make_async_copy(first_hbm, first_ref, moment_sems.at[0])
    second_copy = pltpu.make_async_copy(second_hbm, second_ref, moment_sems.at[1])
    first_copy.start()
    second_copy.start()

    def in_group(step):
        peer = lax.rem(me + step, group_n)
        return peer, {"shard": peer // tensors_n, "tensor": lax.rem(peer, tensors_n)}

    def in_section(step):
        return {"section": lax.rem(section_pos + step, sections_n)}

    barrier = pltpu.get_barrier_semaphore()
    for step in range(1, group_n):
        pl.semaphore_signal(barrier, inc=1, device_id=in_group(step)[1], device_id_type=MESH)
    for step in range(1, sections_n):
        pl.semaphore_signal(barrier, inc=1, device_id=in_section(step), device_id_type=MESH)
    pl.semaphore_wait(barrier, group_n - 1 + sections_n - 1)

    def remote(source, target, sems, k, where):
        return pltpu.make_async_remote_copy(
            src_ref=source,
            dst_ref=target,
            send_sem=sems.at[0, k],
            recv_sem=sems.at[1, k],
            device_id=where,
            device_id_type=MESH,
        )

    gain_squares = gain_ref[...] * gain_ref[...]
    share = jnp.sum(gain_squares) / float(group_n)
    local = jnp.sum(square_ref[...]) + share
    one_square[...] = jnp.full(one_square.shape, local, jnp.float32)
    section_copies = []
    for step in range(1, sections_n):
        copy = remote(
            one_square, section_slots.at[section_pos], section_sems, step, in_section(step)
        )
        copy.start()
        section_copies.append(copy)
    section_slots[section_pos] = one_square[...]

    row_copies = []
    for step in range(1, tensors_n):
        peer = lax.rem(tensor_pos + step, tensors_n)
        copy = remote(rows_ref.at[peer], row_slots.at[step], row_sems, step, {"tensor": peer})
        copy.start()
        row_copies.append(copy)

    for copy in section_copies:
        copy.wait_recv()
    total = section_slots[0]
    for k in range(1, sections_n):
        total = total + section_slots[k]
    group_square[...] = total
    group_copies = []
    for step in range(1, group_n):
        copy = remote(
            group_square, group_slots.at[me], group_sems, step, in_group(step)[1]
        )
        copy.start()
        group_copies.append(copy)
    group_slots[me] = group_square[...]
    for copy in group_copies:
        copy.wait_recv()
    total = group_slots[0]
    for k in range(1, group_n):
        total = total + group_slots[k]
    clip_tile = jnp.minimum(1.0, lax.rsqrt(total / entry_count + clip_eps))
    clip = clip_tile[0:1, 0:1]

    first_copy.wait()
    second_copy.wait()

    def dir_copy(c):
        columns = pl.ds(pl.multiple_of(c * width, width), width)
        return remote(
            dir_own.at[:, columns],
            dir_landed.at[:, columns],
            dir_sems,
            c,
            {"shard": 1 - shard_pos},
        )

    @pl.loop(0, chunks)
    def _(c):
        columns = pl.ds(pl.multiple_of(c * width, width), width)
        rows = pl.ds(pl.multiple_of(shard_pos * rank_rows, rank_rows), rank_rows)
        first_new, second_new, direction = adam_direction(
            clip * proj_ref[c, rows, :], first_ref[:, columns], second_ref[:, columns]
        )
        first_out[:, columns] = first_new
        second_out[:, columns] = second_new
        dir_own[:, columns] = direction
        dir_copy(c).start()

    first_new, second_new, direction = adam_direction(
        clip * gain_ref[shard_pos], gain_first_ref[...], gain_second_ref[...]
    )
    gain_first_out[...] = first_new
    gain_second_out[...] = second_new
    gain_step_out[...] = direction

    for copy in row_copies:
        copy.wait_recv()
    current = rows_ref[tensor_pos]
    for step in range(1, tensors_n):
        current = current + row_slots[step]
    gram[...] = exact_dims(current, current, ((0,), (0,)))
    gram_copies = []
    for step in range(1, group_n):
        peer, where = in_group(step)
        copy = remote(
            gram.at[pl.ds(pl.multiple_of(peer * piece, piece), piece), :],
            gram_slots.at[step],
            gram_sems,
            step,
            where,
        )
        copy.start()
        gram_copies.append(copy)
    mine = pl.ds(pl.multiple_of(me * piece, piece), piece)
    summed = gram[mine, :]
    for step, copy in enumerate(gram_copies):
        copy.wait_recv()
        summed = summed + gram_slots[step + 1]
    gram_part[...] = summed
    full_copies = []
    for step in range(1, group_n):
        copy = remote(gram_part, gram_full.at[mine, :], full_sems, step, in_group(step)[1])
        copy.start()
        full_copies.append(copy)
    gram_full[mine, :] = summed
    for copy in full_copies:
        copy.wait_recv()
    mixer, scale = ns_mixer(gram_full[...])
    basis_out[...] = exact_dot(current * scale, mixer)

    @pl.loop(0, chunks)
    def _(c):
        dir_copy(c).wait_recv()
        dir_copy(c).wait_send()

    direction_out[shard_pos] = dir_own[...]
    direction_out[1 - shard_pos] = dir_landed[...]
    for copies in (section_copies, row_copies, group_copies, gram_copies, full_copies):
        for copy in copies:
            copy.wait_send()


def finish(axes, proj, rows, square, gain, first, second, gain_first, gain_second):
    shards_n, tensors_n, sections_n, _ = axes
    group_n = shards_n * tensors_n
    chunks, rank, width = proj.shape
    rank_rows, cols = first.shape
    f32 = jnp.float32
    vmem = pl.BlockSpec(memory_space=pltpu.VMEM)
    shape = jax.ShapeDtypeStruct
    tile = (8, 128)
    dma = pltpu.SemaphoreType.DMA
    return pl.pallas_call(
        functools.partial(finish_kernel, axes),
        out_shape=(
            shape((rank_rows, cols), f32),
            shape((rank_rows, cols), f32),
            shape((shards_n, rank_rows, cols), f32),
            shape((rank, rank), f32),
            shape(gain_first.shape, f32),
            shape(gain_first.shape, f32),
            shape(gain_first.shape, f32),
        ),
        in_specs=[vmem] * 4 + [pl.BlockSpec(memory_space=pl.ANY)] * 2 + [vmem] * 2,
        out_specs=(vmem,) * 7,
        scratch_shapes=[
            pltpu.VMEM(rows.shape, f32),
            pltpu.VMEM(tile, f32),
            pltpu.VMEM((sections_n,) + tile, f32),
            pltpu.VMEM(tile, f32),
            pltpu.VMEM((group_n,) + tile, f32),
            pltpu.VMEM((rank_rows, cols), f32),
            pltpu.VMEM((rank_rows, cols), f32),
            pltpu.VMEM((rank, rank), f32),
            pltpu.VMEM((group_n, rank // group_n, rank), f32),
            pltpu.VMEM((rank // group_n, rank), f32),
            pltpu.VMEM((rank, rank), f32),
            dma((2, tensors_n)),
            dma((2, sections_n)),
            dma((2, group_n)),
            dma((2, chunks)),
            dma((2, group_n)),
            dma((2, group_n)),
            pltpu.VMEM(first.shape, f32),
            pltpu.VMEM(second.shape, f32),
            dma((2,)),
        ],
        compiler_params=pltpu.CompilerParams(
            collective_id=1, has_side_effects=True, vmem_limit_bytes=48 * 2**20
        ),
        cost_estimate=pl.CostEstimate(flops=2**32, bytes_accessed=2**24, transcendentals=2**20),
        name="finish",
    )(proj, rows, square, gain, first, second, gain_first, gain_second)


def split(value):
    high = value.astype(jnp.bfloat16)
    return high, (value - high.astype(jnp.float32)).astype(jnp.bfloat16)


def apply_kernel(basis_ref, direction_ref, *refs):
    count = len(refs) // 2
    left_high, left_low = split(basis_ref[...])
    right_high, right_low = split(direction_ref[...])

    def term(left, right):
        return jnp.dot(left, right, preferred_element_type=jnp.float32)

    refs[count][...] = (
        term(left_low, right_high) + term(left_high, right_low) + term(left_high, right_high)
    )
    for source, target in zip(refs[:count], refs[count + 1 :]):
        target[...] = source[...]


def apply_direction(basis_here, direction, moments, rest):
    rows_here, rank = basis_here.shape
    cols = direction.shape[1]
    f32 = jnp.float32

    def by_column(shape):
        return pl.BlockSpec((shape[0], CHUNK), lambda c: (0, c))

    def whole(shape):
        return pl.BlockSpec(shape, lambda c: (0, 0))

    passed = [by_column(a.shape) for a in moments] + [whole(a.shape) for a in rest]
    arrays = list(moments) + list(rest)
    shape = jax.ShapeDtypeStruct
    return pl.pallas_call(
        apply_kernel,
        grid=(cols // CHUNK,),
        out_shape=[shape((rows_here, cols), f32)] + [shape(a.shape, f32) for a in arrays],
        in_specs=[whole(basis_here.shape), by_column(direction.shape)] + passed,
        out_specs=[by_column((rows_here, cols))] + passed,
        compiler_params=pltpu.CompilerParams(vmem_limit_bytes=32 * 2**20),
        name="apply_direction",
    )(basis_here, direction, *arrays)


def paired(
    activations, out_grad, basis, first_moment, second_moment, gain_partial, gain_first, gain_second
):
    shards_n = lax.axis_size("shard")
    tensors_n = lax.axis_size("tensor")
    sections_n = lax.axis_size("section")
    rows_here = basis.shape[1]
    rank = basis.shape[2]
    cols = out_grad.shape[2]
    basis_here = basis[0]
    gain = gain_partial[0, 0].reshape(shards_n, 8, rows_here // 8)
    proj, rows, square, gain_total = exchange(activations[0], out_grad[0], basis_here.T, gain)
    axes = (shards_n, tensors_n, sections_n, float(sections_n * (D * FF + D)))
    gain_shape = (8, rows_here // 8)
    first, second, direction, new_basis, gain_step, gain_first_new, gain_second_new = finish(
        axes,
        proj,
        rows.reshape(tensors_n, rows_here // tensors_n, rank),
        square,
        gain_total,
        first_moment[0],
        second_moment[0],
        gain_first[0].reshape(gain_shape),
        gain_second[0].reshape(gain_shape),
    )
    update, first, second, new_basis, gain_step, gain_first_new, gain_second_new = apply_direction(
        basis_here,
        direction.reshape(rank, cols),
        (first, second),
        (new_basis, gain_step, gain_first_new, gain_second_new),
    )
    return (
        update[None],
        first[None],
        second[None],
        new_basis[None],
        gain_step.reshape(1, rows_here),
        gain_first_new.reshape(1, rows_here),
        gain_second_new.reshape(1, rows_here),
    )


def solution(mesh):
    placed = (
        P("section", "shard", None),
        P("section", "shard", "tensor"),
        P("section", "shard", None),
        P("section", "shard", "tensor"),
        P("section", "shard", "tensor"),
        P("section", "shard", None),
        P("section", "shard"),
        P("section", "shard"),
    )
    one_layer = mesh.shape["section"] == LAYERS
    body = paired if mesh.shape["shard"] == 2 and one_layer else shards
    return jax.shard_map(
        body,
        mesh=mesh,
        in_specs=placed,
        out_specs=(
            P("section", "shard", "tensor"),
            P("section", "shard", "tensor"),
            P("section", "shard", "tensor"),
            P("section", ("shard", "tensor"), None),
            P("section", "shard"),
            P("section", "shard"),
            P("section", "shard"),
        ),
        check_vma=False,
    )
```
